32 devices in a mesh: tile: 16 (over z, y, x), rep: 2 (over core).
Axes of the slice: x: 2, y: 2, z: 4, core: 2. Of those that a mesh axis runs over, the one named last changes fastest.
Arguments:
- fields: bfloat16 [2, 16, 16, 16, 256], P('rep', 'tile'), may hold values from -6 to 6
- upstream: bfloat16 [2, 16, 16, 16, 256], P('rep', 'tile'), may hold values from -6 to 6
- kernel: float32 [7, 7, 256], replicated, may hold values from -0.875 to 0.875
- gain: float32 [256], replicated, may hold values from 0.1 to 1.9
- w_up: bfloat16 [256, 1024], replicated, may hold values from -0.375 to 0.375
- w_down: bfloat16 [1024, 256], replicated, may hold values from -0.1875 to 0.1875
- scale: float32 [256], replicated, may hold values from 0.1 to 1
- spins: int32 [16], replicated, may hold values from 0 to 3
- corner_counts: int32 [16, 4], replicated, may hold values 0 or 1
Outputs:
- field_grad: bfloat16 [2, 16, 16, 16, 256], P('rep', 'tile')
- kernel_grad: float32 [7, 7, 256], replicated
- gain_grad: float32 [256], replicated
- up_grad: float32 [256, 1024], replicated
- down_grad: float32 [1024, 256], replicated
- scale_grad: float32 [256], replicated
The draws below stay inside these ranges and needn't reach their ends.
All inputs are finite; a program needn't handle non-finite values.
Results may differ from the reference program's by a relative error of at most 0.0067.
Values may be sent and summed in bfloat16 or wider, within the bound.
A program may use at most 64 MiB of HBM per device.

```python
import math
import jax
import jax.numpy as jnp
from jax import lax

C = 256
FF = 1024
KS = 7
S = 16
TILES = 16
BATCH = 2


def place_ends(values, rng, least, high):
    shape = values.shape
    place = [jax.random.randint(jax.random.fold_in(rng, axis), (), 0, shape[axis]) for axis in range(len(shape))]
    values = values.at[tuple(place)].set(least)
    longest = shape.index(max(shape))
    place[longest] = (place[longest] + 1) % shape[longest]
    return values.at[tuple(place)].set(high)


def shard_levels(own_key, extent, pieces, low, largest):
    def one(axis_at, blocks):
        heights = jax.random.uniform(jax.random.fold_in(jax.random.fold_in(own_key, 6), axis_at), (blocks,), jnp.float32, low / len(pieces), largest / len(pieces))
        return jnp.repeat(jnp.exp(heights), extent[axis_at] // blocks).reshape((-1,) + (1,) * (len(extent) - axis_at - 1))

    level = one(*pieces[0])
    for cut in pieces[1:]:
        level = level * one(*cut)
    return level


def scatter_about(own_key, dims, deviation, limit, pieces=(), kind=jnp.bfloat16):
    values = jax.random.normal(own_key, dims, jnp.float32) * deviation
    if len(pieces) > 0:
        values = shard_levels(own_key, dims, pieces, -0.22, 0.18) * values
    return jnp.clip(values, min=-limit, max=limit).astype(kind)


def setup_inputs(seed: int = 0) -> dict:
    key_of = jax.random.split(jax.random.key(seed), 10)
    return {
        "fields": scatter_about(key_of[0], (BATCH, TILES, S, S, C), 1.0, 6.0, ((0, 2), (1, 16))),
        "upstream": scatter_about(key_of[1], (BATCH, TILES, S, S, C), 1.0, 6.0, ((0, 2), (1, 16))),
        "kernel": scatter_about(key_of[2], (KS, KS, C), (KS * KS) ** -0.5, 0.875, (), jnp.float32),
        "gain": jnp.clip(1.0 + 0.18 * jax.random.normal(key_of[3], (C,), jnp.float32), 0.1, 1.9),
        "w_up": scatter_about(key_of[4], (C, FF), C ** -0.5, 0.375),
        "w_down": scatter_about(key_of[5], (FF, C), FF ** -0.5, 0.1875),
        "scale": jnp.clip(jnp.exp(jax.random.uniform(key_of[6], (C,), jnp.float32, math.log(0.1), math.log(1.0))), 0.1, 1.0),
        "spins": place_ends(jax.random.randint(key_of[7], (TILES,), 0, 4), jax.random.fold_in(key_of[7], 1), 0, 3).astype(jnp.int32),
        "corner_counts": place_ends((jax.random.randint(key_of[8], (TILES, 4), 0, 4) < 3).astype(jnp.int32), jax.random.fold_in(key_of[8], 1), 0, 1),
    }


epsilon = 1e-06
gelu_scale = 0.7978845608028654
gelu_cubic = 0.044715

def rotate(field, quarter):
    return jnp.rot90(field, quarter, axes=(-3, -2))

def edge_strips(field):
    return jnp.stack([rotate(field, side_idx)[..., :3, :, :] for side_idx in range(4)], axis=-4)

def corner_blocks(field):
    return jnp.stack([rotate(field, side_idx)[..., :3, :3, :] for side_idx in range(4)], axis=-4)

def glue_tiles(spins):
    stride = TILES // 2 ** ((TILES.bit_length() - 1) // 2)
    tile_ids = jnp.arange(TILES, dtype=jnp.int32)
    grid_side = (jnp.arange(4, dtype=jnp.int32)[None, :] + spins[:, None]) % 4
    edge_steps = jnp.array([-stride, 1, stride, -1], jnp.int32)
    corner_steps = jnp.array([-stride - 1, -stride + 1, stride + 1, stride - 1], jnp.int32)
    neighbours = ((tile_ids[:, None] + edge_steps[grid_side]) % TILES).astype(jnp.int32)
    facing = ((grid_side + 2 - spins[neighbours]) % 4).astype(jnp.int32)
    corner_tiles = ((tile_ids[:, None] + corner_steps[grid_side]) % TILES).astype(jnp.int32)
    corner_codes = ((grid_side + 2 - spins[corner_tiles]) % 4).astype(jnp.int32)
    return (neighbours, facing, corner_tiles, corner_codes)

def assemble(field, halo_cells, corner_cells):
    widths = [(0, 0)] * (field.ndim - 3) + [(3, 3), (3, 3), (0, 0)]
    padded = jnp.pad(field, widths)
    for side_idx in range(4):
        turned = rotate(padded, side_idx)
        turned = turned.at[..., :3, 3:-3, :].set(halo_cells[..., side_idx, ::-1, :, :])
        turned = turned.at[..., :3, :3, :].set(corner_cells[..., side_idx, ::-1, ::-1, :])
        padded = rotate(turned, -side_idx)
    return padded

def split_padded(grad_pad):
    halo_parts = []
    corner_parts = []
    for side_idx in range(4):
        turned = rotate(grad_pad, side_idx)
        halo_parts.append(turned[..., 2::-1, 3:-3, :])
        corner_parts.append(turned[..., 2::-1, 2::-1, :])
    return (grad_pad[..., 3:-3, 3:-3, :], jnp.stack(halo_parts, axis=-4), jnp.stack(corner_parts, axis=-4))

def strips_back(strip_grads, corner_grads, shape):
    summed = jnp.zeros(shape, jnp.float32)
    for side_idx in range(4):
        turned = rotate(summed, side_idx)
        turned = turned.at[..., :3, :, :].add(strip_grads[..., side_idx, :, :, :])
        turned = turned.at[..., :3, :3, :].add(corner_grads[..., side_idx, :, :, :])
        summed = rotate(turned, -side_idx)
    return summed

def block_grads(padded, upstream, kernel, gain, w_up, w_down, scale):
    side_len = upstream.shape[-2]
    channels = upstream.shape[-1]
    widened = padded.astype(jnp.float32)
    conv_sum = jnp.zeros(upstream.shape, jnp.float32)
    for row_off in range(7):
        for col_off in range(7):
            conv_sum = conv_sum + widened[:, row_off:row_off + side_len, col_off:col_off + side_len, :] * kernel[row_off, col_off]
    chan_mean = lax.optimization_barrier(jnp.mean(conv_sum, axis=-1, keepdims=True))
    centred = conv_sum - chan_mean
    inv_std = lax.rsqrt(lax.optimization_barrier(jnp.mean(centred * centred, axis=-1, keepdims=True)) + epsilon)
    whitened = centred * inv_std
    normed = (whitened * gain).astype(jnp.bfloat16).reshape(-1, channels)
    hidden = jnp.dot(normed, w_up, preferred_element_type=jnp.float32)
    tangent = jnp.tanh(gelu_scale * (hidden + gelu_cubic * hidden * hidden * hidden))
    activated = (0.5 * hidden * (1.0 + tangent)).astype(jnp.bfloat16)
    projected = jnp.dot(activated, w_down, preferred_element_type=jnp.float32)
    upstream_flat = upstream.reshape(-1, channels).astype(jnp.float32)
    g_scale = lax.optimization_barrier(jnp.sum(upstream_flat * projected, axis=0))
    d_out = (upstream_flat * scale).astype(jnp.bfloat16)
    contract_rows = (((0,), (0,)), ((), ()))
    contract_cols = (((1,), (1,)), ((), ()))
    g_down = lax.dot_general(activated, d_out, contract_rows, preferred_element_type=jnp.float32)
    d_act = lax.dot_general(d_out, w_down, contract_cols, preferred_element_type=jnp.float32)
    gelu_slope = 0.5 * (1.0 + tangent) + 0.5 * hidden * (1.0 - tangent * tangent) * gelu_scale * (1.0 + 3.0 * gelu_cubic * hidden * hidden)
    d_hidden = (d_act * gelu_slope).astype(jnp.bfloat16)
    g_up = lax.dot_general(normed, d_hidden, contract_rows, preferred_element_type=jnp.float32)
    d_normed = lax.dot_general(d_hidden, w_up, contract_cols, preferred_element_type=jnp.float32).reshape(conv_sum.shape)
    g_gain = lax.optimization_barrier(jnp.sum(d_normed * whitened, axis=(0, 1, 2)))
    d_white = d_normed * gain
    d_conv = inv_std * (d_white - lax.optimization_barrier(jnp.mean(d_white, axis=-1, keepdims=True)) - whitened * lax.optimization_barrier(jnp.mean(d_white * whitened, axis=-1, keepdims=True)))
    kernel_rows = []
    grad_pad = jnp.zeros(widened.shape, jnp.float32)
    for row_off in range(7):
        kernel_cols = []
        for col_off in range(7):
            window = widened[:, row_off:row_off + side_len, col_off:col_off + side_len, :]
            kernel_cols.append(lax.optimization_barrier(jnp.sum(window * d_conv, axis=(0, 1, 2))))
            grad_pad = grad_pad.at[:, row_off:row_off + side_len, col_off:col_off + side_len, :].add(d_conv * kernel[row_off, col_off])
        kernel_rows.append(jnp.stack(kernel_cols))
    g_kernel = jnp.stack(kernel_rows)
    return (grad_pad, (g_kernel, g_gain, g_up, g_down, g_scale))

def reference(fields, upstream, kernel, gain, w_up, w_down, scale, spins, corner_counts):
    neighbours, facing, corner_tiles, corner_codes = glue_tiles(spins)
    strips = edge_strips(fields)
    blocks = corner_blocks(fields)
    corner_mask = corner_counts.astype(fields.dtype)[None, :, :, None, None, None]
    halo_cells = strips[:, neighbours, facing][..., ::-1, :]
    corner_cells = blocks[:, corner_tiles, corner_codes] * corner_mask

    def flatten(array):
        return array.reshape((BATCH * TILES,) + array.shape[2:])

    def tile_step(running, per_tile):
        tile_field, tile_halo, tile_corner, tile_upstream = per_tile
        padded = assemble(tile_field, tile_halo, tile_corner)[None]
        grad_pad, gradients = block_grads(padded, tile_upstream[None], kernel, gain, w_up, w_down, scale)
        interior, grad_halo, grad_corner = split_padded(grad_pad[0])
        running = tuple((left + right for left, right in zip(running, gradients)))
        return (running, (tile_upstream.astype(jnp.float32) + interior, grad_halo.astype(jnp.bfloat16), grad_corner.astype(jnp.bfloat16)))
    initial = (jnp.zeros((7, 7, C), jnp.float32), jnp.zeros((C,), jnp.float32), jnp.zeros((C, FF), jnp.float32), jnp.zeros((FF, C), jnp.float32), jnp.zeros((C,), jnp.float32))
    grad_sums, outputs = lax.scan(tile_step, initial, (flatten(fields), flatten(halo_cells), flatten(corner_cells), flatten(upstream)))
    residual_part, halo_back, corner_back = outputs
    halo_shaped = halo_back.reshape(strips.shape).astype(jnp.float32)[..., ::-1, :]
    strip_grads = jnp.zeros(strips.shape, jnp.float32).at[:, neighbours, facing].add(halo_shaped)
    corner_shaped = corner_back.reshape(blocks.shape).astype(jnp.float32) * corner_mask.astype(jnp.float32)
    corner_grads = jnp.zeros(blocks.shape, jnp.float32).at[:, corner_tiles, corner_codes].add(corner_shaped)
    field_grad = (residual_part.reshape(fields.shape) + strips_back(strip_grads, corner_grads, fields.shape)).astype(jnp.bfloat16)
    factor = 1.0 / math.sqrt(BATCH * TILES * S * S)
    return (field_grad, grad_sums[0] * factor, grad_sums[1] * factor, grad_sums[2] * factor, grad_sums[3] * factor, grad_sums[4] * factor)
```

```python
import functools
import math

import jax
import jax.numpy as jnp
import numpy as np
from jax import lax
from jax.experimental import pallas as pl
from jax.experimental.pallas import tpu as pltpu
from jax.sharding import PartitionSpec as P

epsilon = 1e-06
gelu_scale = 0.7978845608028654
gelu_cubic = 0.044715
MESH = pl.DeviceIdType.MESH
SIDE = 16
WIDE = 22
PITCH = 24
PIECE = 64
SMALL = 64
PARTS = 2


def tables():
    cells = np.arange(SIDE * SIDE).reshape(SIDE, SIDE)
    pads = np.arange(WIDE * PITCH).reshape(WIDE, PITCH)[:, :WIDE]
    cut = np.zeros((4 * PIECE, SIDE * SIDE), np.float32)
    paste = np.zeros((WIDE * PITCH, 4 * PIECE), np.float32)
    centre = np.zeros((WIDE * PITCH, SIDE * SIDE), np.float32)
    for edge in range(4):
        turned = np.rot90(cells, edge)
        wide = np.rot90(pads, edge)
        for depth in range(3):
            for along in range(SIDE):
                cut[edge * PIECE + depth * SIDE + along, turned[depth, along]] = 1
                paste[wide[2 - depth, 3 + along], edge * PIECE + depth * SIDE + SIDE - 1 - along] = 1
            for along in range(3):
                row = edge * PIECE + 48 + depth * 3 + along
                cut[row, turned[depth, along]] = 1
                paste[wide[2 - depth, 2 - along], row] = 1
    for row in range(SIDE):
        for col in range(SIDE):
            centre[pads[row + 3, col + 3], cells[row, col]] = 1
    return [jnp.asarray(t, jnp.bfloat16) for t in (cut, cut.T, paste, paste.T, centre)]


def plan(tiles, reps, rows):
    groups = []
    if reps > 1:
        groups.append(("rep", 1, reps))
    stride = 1
    while stride < tiles:
        size = 4 if tiles // stride % 4 == 0 else 2
        groups.append(("tile", stride, size))
        stride *= size
    phases = []
    for axis, stride, size in groups:
        scatter = rows % (16 * size) == 0
        out = rows // size if scatter else rows
        phases.append((axis, stride, size, scatter, rows, out))
        rows = out
    return phases


def dot(left, right, dims=((1,), (0,))):
    return lax.dot_general(left, right, (dims, ((), ())), preferred_element_type=jnp.float32)


def body(
    tiles, phases,
    field_ref, up_ref, kern_ref, gain_ref, wup_ref, wdown_ref, scale_ref, spins_ref, counts_ref,
    cut_ref, cut_t_ref, paste_ref, paste_t_ref, centre_ref,
    grad_ref, gup_ref, gdown_ref, gsmall_ref,
    pieces, sent, got, pieces_b, sent_b, got_b, turned,
    pad_ref, shift_ref, conv_ref, dact_ref, dcp_ref, dpad_ref, gbuf, agbuf, small_ref,
    send_sem, recv_sem, *bufs,
):
    count = len(phases)
    recv_bufs = bufs[:count]
    red_bufs = bufs[count : 2 * count]
    small_bufs = bufs[2 * count : 3 * count]
    tile = lax.axis_index("tile")
    rep = lax.axis_index("rep")
    side = tiles // 2 ** ((tiles.bit_length() - 1) // 2)
    steps = [-side, 1, side, -1, -side - 1, -side + 1, side + 1, side - 1]

    def across(step):
        return {"tile": lax.rem(tile + step + tiles, tiles)}

    def place(phase):
        axis, stride, size = phases[phase][:3]
        return rep if axis == "rep" else lax.rem(tile // stride, size)

    def member(phase, ahead):
        axis, stride, size = phases[phase][:3]
        pos = place(phase)
        other = lax.rem(pos + ahead, size)
        if axis == "rep":
            return {"rep": other}, other
        return {"tile": tile + (other - pos) * stride}, other

    barrier = pltpu.get_barrier_semaphore()
    greeted = 0
    for step in steps:
        pl.semaphore_signal(barrier, inc=1, device_id=across(step), device_id_type=MESH)
        greeted += 1
    for phase in range(count):
        for ahead in range(1, phases[phase][2]):
            pl.semaphore_signal(
                barrier, inc=1, device_id=member(phase, ahead)[0], device_id_type=MESH
            )
            greeted += 1

    used = [0]
    started = []

    def push(src, dst, device):
        slot = used[0]
        used[0] += 1
        copy = pltpu.make_async_remote_copy(
            src_ref=src, dst_ref=dst, send_sem=send_sem.at[slot], recv_sem=recv_sem.at[slot],
            device_id=device, device_id_type=MESH,
        )
        copy.start()
        started.append(copy)
        return copy

    spin = spins_ref[tile]
    is_corner = lax.broadcasted_iota(jnp.int32, (PIECE, 256), 0) >= 48

    def masked(piece, edge):
        keep = jnp.where(is_corner, counts_ref[tile, edge].astype(jnp.float32), 1.0)
        return (piece.astype(jnp.float32) * keep).astype(jnp.bfloat16)

    def trade(source, out, into):
        for grid in range(4):
            out[grid] = source[lax.rem(grid - spin + 4, 4)]
        copies = []
        for grid in range(4):
            copies.append(push(out.at[grid, pl.ds(0, 48)], into.at[(grid + 2) % 4, pl.ds(0, 48)], across(steps[grid])))
        for grid in range(4):
            copies.append(push(out.at[grid, pl.ds(48, 16)], into.at[(grid + 2) % 4, pl.ds(48, 16)], across(steps[4 + grid])))
        return copies

    flying = [None] * PARTS
    reached = [0] * PARTS
    offsets = []
    offset = 0
    for phase in range(count):
        if phases[phase][3]:
            offset = offset + place(phase) * phases[phase][5]
        offsets.append(offset)

    def source_of(part, phase):
        return gbuf.at[part] if phase == 0 else red_bufs[phase - 1].at[part]

    def begin(part):
        phase = reached[part]
        size, scatter, rows, out = phases[phase][2:]
        src = source_of(part, phase)
        copies = []
        if not scatter:
            recv_bufs[phase][part, place(phase)] = src[...]
        for ahead in range(1, size):
            device, other = member(phase, ahead)
            if scatter:
                start = pl.multiple_of(other * out, 16)
                copies.append(push(src.at[pl.ds(start, out)], recv_bufs[phase].at[part, ahead - 1], device))
            else:
                copies.append(push(src, recv_bufs[phase].at[part, place(phase)], device))
        flying[part] = copies

    def finish(part):
        phase = reached[part]
        size, scatter, rows, out = phases[phase][2:]
        src = source_of(part, phase)
        for copy in flying[part]:
            copy.wait_recv()
        if scatter:
            total = src[pl.ds(pl.multiple_of(place(phase) * out, 16), out)].astype(jnp.float32)
            for slot in range(size - 1):
                total = total + recv_bufs[phase][part, slot].astype(jnp.float32)
        else:
            total = recv_bufs[phase][part, 0].astype(jnp.float32)
            for slot in range(1, size):
                total = total + recv_bufs[phase][part, slot].astype(jnp.float32)
        reached[part] += 1
        if reached[part] < count:
            red_bufs[phase][part] = total.astype(jnp.bfloat16)
        else:
            agbuf[part, pl.ds(pl.multiple_of(offsets[-1], 16), out)] = total.astype(jnp.bfloat16)

    def advance(part):
        if reached[part] < count:
            finish(part)
            if reached[part] < count:
                begin(part)

    def gather(part, phase):
        size, scatter, rows, out = phases[phase][2:]
        if not scatter:
            return []
        here = agbuf.at[part, pl.ds(pl.multiple_of(offsets[phase], 16), out)]
        return [push(here, here, member(phase, ahead)[0]) for ahead in range(1, size)]

    pieces[...] = dot(cut_ref[...], field_ref[...]).astype(jnp.bfloat16).reshape(4, PIECE, 256)
    pl.semaphore_wait(barrier, greeted)
    copies = trade(pieces, sent, got)
    upstream = up_ref[...].astype(jnp.float32)
    d_out = (upstream * scale_ref[...]).astype(jnp.bfloat16)
    for block in range(4):
        cols = pl.ds(block * 256, 256)
        dact_ref[:, cols] = dot(d_out, wdown_ref[cols, :], ((1,), (1,)))
    inner = dot(centre_ref[...], field_ref[...])
    dcp_ref[0:6] = jnp.zeros((6, SIDE, 256), jnp.float32)
    dcp_ref[WIDE : WIDE + 6] = jnp.zeros((6, SIDE, 256), jnp.float32)
    small_ref[...] = jnp.zeros((SMALL, 256), jnp.float32)
    for copy in copies:
        copy.wait_recv()
    for edge in range(4):
        turned[pl.ds(edge * PIECE, PIECE), :] = masked(got[lax.rem(edge + spin, 4)], edge)
    pad_ref[...] = (inner + dot(paste_ref[...], turned[...])).reshape(WIDE, PITCH, 256)
    for col in range(7):
        shift_ref[col] = pad_ref[:, pl.ds(col, SIDE), :]

    @pl.loop(0, SIDE // 4)
    def _(group):
        acc = [jnp.zeros((SIDE, 256), jnp.float32) for _ in range(4)]
        for col in range(7):
            for row in range(7):
                tap = kern_ref[pl.ds(row * 7 + col, 1), :]
                for line in range(4):
                    acc[line] = acc[line] + shift_ref[col, group * 4 + line + row] * tap
        for line in range(4):
            conv_ref[group * 4 + line] = acc[line]

    conv = conv_ref[...].reshape(SIDE * SIDE, 256)
    gain = gain_ref[...]
    centred = conv - jnp.mean(conv, axis=1, keepdims=True)
    inv_std = lax.rsqrt(jnp.mean(centred * centred, axis=1, keepdims=True) + epsilon)
    whitened = centred * inv_std
    normed = (whitened * gain).astype(jnp.bfloat16)
    projected = jnp.zeros((SIDE * SIDE, 256), jnp.float32)
    d_normed = jnp.zeros((SIDE * SIDE, 256), jnp.float32)
    per_part = 4 // PARTS
    for block in range(4):
        cols = pl.ds(block * 256, 256)
        part, local = block // per_part, block % per_part
        h = dot(normed, wup_ref[:, cols])
        square = h * h
        t = jnp.tanh(gelu_scale * h * (1.0 + gelu_cubic * square))
        half = 0.5 * (1.0 + t)
        activated = (h * half).astype(jnp.bfloat16)
        slope = half + 0.5 * h * (1.0 - t * t) * (gelu_scale * (1.0 + 3.0 * gelu_cubic * square))
        d_hidden = (dact_ref[:, cols] * slope).astype(jnp.bfloat16)
        gbuf[part, pl.ds(local * 512, 256)] = dot(normed, d_hidden, ((0,), (0,))).astype(jnp.bfloat16)
        gbuf[part, pl.ds(local * 512 + 256, 256)] = dot(activated, d_out, ((0,), (0,))).astype(jnp.bfloat16)
        if local == per_part - 1:
            begin(part)
        projected = projected + dot(activated, wdown_ref[cols, :])
        d_normed = d_normed + dot(d_hidden, wup_ref[:, cols], ((1,), (1,)))
    for part in range(PARTS - 1):
        advance(part)

    small_ref[49:50, :] = jnp.sum(d_normed * whitened, axis=0, keepdims=True)
    small_ref[50:51, :] = jnp.sum(upstream * projected, axis=0, keepdims=True)
    d_white = d_normed * gain
    d_conv = inv_std * (
        d_white
        - jnp.mean(d_white, axis=1, keepdims=True)
        - whitened * jnp.mean(d_white * whitened, axis=1, keepdims=True)
    )
    dcp_ref[6:WIDE] = d_conv.reshape(SIDE, SIDE, 256)
    advance(PARTS - 1)

    @pl.loop(0, WIDE // 2)
    def _(group):
        total = [jnp.zeros((PITCH, 256), jnp.float32) for _ in range(2)]
        for col in range(7):
            acc = [jnp.zeros((SIDE, 256), jnp.float32) for _ in range(2)]
            for row in range(7):
                tap = kern_ref[pl.ds(row * 7 + col, 1), :]
                for line in range(2):
                    acc[line] = acc[line] + dcp_ref[group * 2 + line + 6 - row] * tap
            for line in range(2):
                long = jnp.concatenate([acc[line], jnp.zeros((8, 256), jnp.float32)], axis=0)
                total[line] = total[line] + (pltpu.roll(long, col, 0) if col else long)
        for line in range(2):
            dpad_ref[group * 2 + line] = total[line]

    rounded = dpad_ref[...].reshape(WIDE * PITCH, 256).astype(jnp.bfloat16)
    back = dot(paste_t_ref[...], rounded).astype(jnp.bfloat16)
    for edge in range(4):
        pieces_b[edge] = masked(back[edge * PIECE : (edge + 1) * PIECE], edge)
    copies = trade(pieces_b, sent_b, got_b)
    for part in range(PARTS):
        advance(part)

    for col in range(7):
        def line_sum(line, acc, col=col):
            grads = dcp_ref[line + 6]
            return tuple(acc[row] + shift_ref[col, line + row] * grads for row in range(7))

        sums = lax.fori_loop(
            0, SIDE, line_sum, tuple(jnp.zeros((SIDE, 256), jnp.float32) for _ in range(7))
        )
        for row in range(7):
            small_ref[pl.ds(row * 7 + col, 1), :] = jnp.sum(sums[row], axis=0, keepdims=True)

    def small_begin(phase):
        own = small_bufs[phase].at[place(phase)]
        own[...] = small_ref[...].astype(jnp.bfloat16)
        return [push(own, own, member(phase, ahead)[0]) for ahead in range(1, phases[phase][2])]

    def small_finish(phase, copies):
        for copy in copies:
            copy.wait_recv()
        total = small_bufs[phase][0].astype(jnp.float32)
        for slot in range(1, phases[phase][2]):
            total = total + small_bufs[phase][slot].astype(jnp.float32)
        small_ref[...] = total

    small_copies = small_begin(count - 1)
    for _ in range(count):
        for part in range(PARTS):
            advance(part)
    gathers = [gather(part, count - 1) for part in range(PARTS)]

    for copy in copies:
        copy.wait_recv()
    for edge in range(4):
        turned[pl.ds(edge * PIECE, PIECE), :] = got_b[lax.rem(edge + spin, 4)]
    inside = dpad_ref[3 : 3 + SIDE, 3 : 3 + SIDE, :].reshape(SIDE * SIDE, 256)
    home = dot(cut_t_ref[...], turned[...])
    grad_ref[...] = (upstream + inside + home).astype(jnp.bfloat16)

    for phase in range(count - 1, -1, -1):
        small_finish(phase, small_copies)
        if phase > 0:
            small_copies = small_begin(phase - 1)
        for part in range(PARTS):
            for copy in gathers[part]:
                copy.wait_recv()
            if phase > 0:
                gathers[part] = gather(part, phase - 1)
    for block in range(4):
        part, local = block // per_part, block % per_part
        gup_ref[:, pl.ds(block * 256, 256)] = agbuf[part, pl.ds(local * 512, 256)]
        gdown_ref[pl.ds(block * 256, 256), :] = agbuf[part, pl.ds(local * 512 + 256, 256)]
    gsmall_ref[...] = small_ref[...]
    for copy in started:
        copy.wait_send()


def on_device(tiles, reps, fields, upstream, kernel, gain, w_up, w_down, scale, spins, corner_counts):
    rows = 2048 // PARTS
    phases = plan(tiles, reps, rows)
    bf16, f32 = jnp.bfloat16, jnp.float32
    per_part = sum(size - 1 for _, _, size, _, _, _ in phases)
    sems = 16 + per_part * (2 * PARTS + 1)
    piece = pltpu.VMEM((4, PIECE, 256), bf16)
    scratch = [
        piece, piece, piece, piece, piece, piece,
        pltpu.VMEM((4 * PIECE, 256), bf16),
        pltpu.VMEM((WIDE, PITCH, 256), f32),
        pltpu.VMEM((7, WIDE, SIDE, 256), f32),
        pltpu.VMEM((SIDE, SIDE, 256), f32),
        pltpu.VMEM((SIDE * SIDE, 1024), f32),
        pltpu.VMEM((WIDE + 6, SIDE, 256), f32),
        pltpu.VMEM((WIDE, PITCH, 256), f32),
        pltpu.VMEM((PARTS, rows, 256), bf16),
        pltpu.VMEM((PARTS, rows, 256), bf16),
        pltpu.VMEM((SMALL, 256), f32),
        pltpu.SemaphoreType.DMA((sems,)),
        pltpu.SemaphoreType.DMA((sems,)),
    ]
    for _, _, size, scatter, _, out in phases:
        scratch.append(pltpu.VMEM((PARTS, size - 1 if scatter else size, out, 256), bf16))
    for _, _, size, scatter, _, out in phases:
        scratch.append(pltpu.VMEM((PARTS, out, 256), bf16))
    for _, _, size, _, _, _ in phases:
        scratch.append(pltpu.VMEM((size, SMALL, 256), bf16))
    vmem = pl.BlockSpec(memory_space=pltpu.VMEM)
    smem = pl.BlockSpec(memory_space=pltpu.SMEM)
    grad, gup, gdown, gsmall = pl.pallas_call(
        functools.partial(body, tiles, phases),
        out_shape=[
            jax.ShapeDtypeStruct((SIDE * SIDE, 256), bf16),
            jax.ShapeDtypeStruct((256, 1024), bf16),
            jax.ShapeDtypeStruct((1024, 256), bf16),
            jax.ShapeDtypeStruct((SMALL, 256), f32),
        ],
        in_specs=[vmem] * 7 + [smem] * 2 + [vmem] * 5,
        out_specs=[vmem] * 4,
        scratch_shapes=scratch,
        compiler_params=pltpu.CompilerParams(
            collective_id=0, has_side_effects=True, vmem_limit_bytes=48 * 2**20
        ),
        cost_estimate=pl.CostEstimate(flops=10**9, bytes_accessed=8 * 2**20, transcendentals=2**18),
        name="block",
    )(
        fields.reshape(SIDE * SIDE, 256), upstream.reshape(SIDE * SIDE, 256),
        kernel.reshape(49, 256), gain.reshape(1, 256), w_up, w_down, scale.reshape(1, 256),
        spins, corner_counts, *tables(),
    )
    factor = 1.0 / math.sqrt(tiles * reps * SIDE * SIDE)
    return (
        grad.reshape(fields.shape),
        gsmall[:49].reshape(7, 7, 256) * factor,
        gsmall[49] * factor,
        gup.astype(f32) * factor,
        gdown.astype(f32) * factor,
        gsmall[50] * factor,
    )


def solution(mesh):
    spread = P("rep", "tile", None, None, None)
    return jax.shard_map(
        functools.partial(on_device, mesh.shape["tile"], mesh.shape["rep"]),
        mesh=mesh,
        in_specs=(spread, spread) + (P(),) * 7,
        out_specs=(spread,) + (P(),) * 5,
        check_vma=False,
    )
```

```python
import functools
import math

import jax
import jax.numpy as jnp
import numpy as np
from jax import lax
from jax.experimental import pallas as pl
from jax.experimental.pallas import tpu as pltpu
from jax.sharding import PartitionSpec as P

epsilon = 1e-06
gelu_scale = 0.7978845608028654
gelu_cubic = 0.044715
MESH = pl.DeviceIdType.MESH
SIDE = 16
WIDE = 22
PITCH = 24
PIECE = 64
SMALL = 64
PARTS = 4
BACKWARDS = (1,)
ARGS = (
    "field", "up", "kern", "gain", "wup", "wdown", "scale", "spins", "counts",
    "cut", "cut_t", "paste", "paste_t", "centre",
)
LOADS = (
    "field", "cut", "spins", "up", "scale", "wdown", "centre", "counts", "paste", "kern",
    "gain", "wup", "paste_t", "cut_t",
)


def tables():
    cells = np.arange(SIDE * SIDE).reshape(SIDE, SIDE)
    pads = np.arange(WIDE * PITCH).reshape(WIDE, PITCH)[:, :WIDE]
    cut = np.zeros((4 * PIECE, SIDE * SIDE), np.float32)
    paste = np.zeros((WIDE * PITCH, 4 * PIECE), np.float32)
    centre = np.zeros((WIDE * PITCH, SIDE * SIDE), np.float32)
    for edge in range(4):
        turned = np.rot90(cells, edge)
        wide = np.rot90(pads, edge)
        for depth in range(3):
            for along in range(SIDE):
                cut[edge * PIECE + depth * SIDE + along, turned[depth, along]] = 1
                paste[wide[2 - depth, 3 + along], edge * PIECE + depth * SIDE + SIDE - 1 - along] = 1
            for along in range(3):
                row = edge * PIECE + 48 + depth * 3 + along
                cut[row, turned[depth, along]] = 1
                paste[wide[2 - depth, 2 - along], row] = 1
    for row in range(SIDE):
        for col in range(SIDE):
            centre[pads[row + 3, col + 3], cells[row, col]] = 1
    return [jnp.asarray(t, jnp.bfloat16) for t in (cut, cut.T, paste, paste.T, centre)]


def plan(tiles, reps, rows, backwards=False):
    groups = []
    if reps > 1:
        groups.append(("rep", 1, reps))
    stride = 1
    while stride < tiles:
        size = 4 if tiles // stride % 4 == 0 else 2
        groups.append(("tile", stride, size))
        stride *= size
    if backwards:
        groups = [g for g in groups if g[0] == "rep"] + [g for g in groups if g[0] != "rep"][::-1]
    phases = []
    for axis, stride, size in groups:
        scatter = rows % (16 * size) == 0
        out = rows // size if scatter else rows
        phases.append((axis, stride, size, scatter, rows, out))
        rows = out
    return phases


def dot(left, right, dims=((1,), (0,))):
    return lax.dot_general(left, right, (dims, ((), ())), preferred_element_type=jnp.float32)


def body(
    tiles, plans,
    *refs,
):
    sources, refs = refs[:14], refs[14:]
    outputs, refs = refs[:4], refs[4:]
    held, load_sem, refs = refs[:14], refs[14], refs[15:]
    loads = {}
    for name in LOADS:
        slot = ARGS.index(name)
        loads[name] = pltpu.make_async_copy(sources[slot], held[slot], load_sem.at[slot])
        loads[name].start()

    def need(*names):
        for name in names:
            loads[name].wait()

    work(tiles, plans, need, *held, *outputs, *refs)


def work(
    tiles, plans, need,
    field_ref, up_ref, kern_ref, gain_ref, wup_ref, wdown_ref, scale_ref, spins_ref, counts_ref,
    cut_ref, cut_t_ref, paste_ref, paste_t_ref, centre_ref,
    grad_ref, gup_ref, gdown_ref, gsmall_ref,
    pieces, sent, got, pieces_b, sent_b, got_b, turned,
    pad_ref, shift_ref, conv_ref, dact_ref, dcp_ref, dpad_ref, gbuf, agbuf, small_ref,
    send_sem, recv_sem, *bufs,
):
    phases = plans[0]
    count = len(phases)
    recv_bufs = [bufs[part * count : (part + 1) * count] for part in range(PARTS)]
    bufs = bufs[PARTS * count :]
    red_bufs = [bufs[part * count : (part + 1) * count] for part in range(PARTS)]
    small_bufs = bufs[PARTS * count :]
    tile = lax.axis_index("tile")
    rep = lax.axis_index("rep")
    side = tiles // 2 ** ((tiles.bit_length() - 1) // 2)
    steps = [-side, 1, side, -1, -side - 1, -side + 1, side + 1, side - 1]

    def across(step):
        return {"tile": lax.rem(tile + step + tiles, tiles)}

    def place(phase, phases=phases):
        axis, stride, size = phases[phase][:3]
        return rep if axis == "rep" else lax.rem(tile // stride, size)

    def member(phase, ahead, phases=phases):
        axis, stride, size = phases[phase][:3]
        pos = place(phase, phases)
        other = lax.rem(pos + ahead, size)
        if axis == "rep":
            return {"rep": other}, other
        return {"tile": tile + (other - pos) * stride}, other

    barrier = pltpu.get_barrier_semaphore()
    greeted = 0
    for step in steps:
        pl.semaphore_signal(barrier, inc=1, device_id=across(step), device_id_type=MESH)
        greeted += 1
    for phase in range(count):
        for ahead in range(1, phases[phase][2]):
            pl.semaphore_signal(
                barrier, inc=1, device_id=member(phase, ahead)[0], device_id_type=MESH
            )
            greeted += 1

    used = [0]
    started = []

    def push(src, dst, device):
        slot = used[0]
        used[0] += 1
        copy = pltpu.make_async_remote_copy(
            src_ref=src, dst_ref=dst, send_sem=send_sem.at[slot], recv_sem=recv_sem.at[slot],
            device_id=device, device_id_type=MESH,
        )
        copy.start()
        started.append(copy)
        return copy

    is_corner = lax.broadcasted_iota(jnp.int32, (PIECE, 256), 0) >= 48

    def masked(piece, edge):
        keep = jnp.where(is_corner, keeps[edge : edge + 1, :], 1.0)
        return (piece.astype(jnp.float32) * keep).astype(jnp.bfloat16)

    def trade(source, out, into, spin):
        for grid in range(4):
            out[grid] = source[lax.rem(grid - spin + 4, 4)]
        copies = []
        for grid in range(4):
            copies.append(push(out.at[grid, pl.ds(0, 48)], into.at[(grid + 2) % 4, pl.ds(0, 48)], across(steps[grid])))
        for grid in range(4):
            copies.append(push(out.at[grid, pl.ds(48, 16)], into.at[(grid + 2) % 4, pl.ds(48, 16)], across(steps[4 + grid])))
        return copies

    flying = [None] * PARTS
    reached = [0] * PARTS
    offsets = []
    for ways in plans:
        offset = 0
        offsets.append([])
        for phase in range(count):
            if ways[phase][3]:
                offset = offset + place(phase, ways) * ways[phase][5]
            offsets[-1].append(offset)

    def source_of(part, phase):
        return gbuf.at[part] if phase == 0 else red_bufs[part][phase - 1]

    def begin(part):
        phase, ways = reached[part], plans[part]
        size, scatter, rows, out = ways[phase][2:]
        src = source_of(part, phase)
        copies = []
        if not scatter:
            recv_bufs[part][phase][place(phase, ways)] = src[...]
        for ahead in range(1, size):
            device, other = member(phase, ahead, ways)
            if scatter:
                start = pl.multiple_of(other * out, 16)
                copies.append(push(src.at[pl.ds(start, out)], recv_bufs[part][phase].at[ahead - 1], device))
            else:
                copies.append(push(src, recv_bufs[part][phase].at[place(phase, ways)], device))
        flying[part] = copies

    def finish(part):
        phase, ways = reached[part], plans[part]
        size, scatter, rows, out = ways[phase][2:]
        src = source_of(part, phase)
        for copy in flying[part]:
            copy.wait_recv()
        if scatter:
            total = src[pl.ds(pl.multiple_of(place(phase, ways) * out, 16), out)].astype(jnp.float32)
            for slot in range(size - 1):
                total = total + recv_bufs[part][phase][slot].astype(jnp.float32)
        else:
            total = recv_bufs[part][phase][0].astype(jnp.float32)
            for slot in range(1, size):
                total = total + recv_bufs[part][phase][slot].astype(jnp.float32)
        reached[part] += 1
        if reached[part] < count:
            red_bufs[part][phase][...] = total.astype(jnp.bfloat16)
        else:
            agbuf[part, pl.ds(pl.multiple_of(offsets[part][-1], 16), out)] = total.astype(jnp.bfloat16)

    def advance(part):
        if reached[part] < count:
            finish(part)
            if reached[part] < count:
                begin(part)

    def gather(part, phase):
        ways = plans[part]
        size, scatter, rows, out = ways[phase][2:]
        if not scatter:
            return []
        here = agbuf.at[part, pl.ds(pl.multiple_of(offsets[part][phase], 16), out)]
        return [push(here, here, member(phase, ahead, ways)[0]) for ahead in range(1, size)]

    need("field", "cut", "spins")
    spin = spins_ref[tile]
    pieces[...] = dot(cut_ref[...], field_ref[...]).astype(jnp.bfloat16).reshape(4, PIECE, 256)
    pl.semaphore_wait(barrier, greeted)
    copies = trade(pieces, sent, got, spin)
    need("up", "scale", "wdown")
    upstream = up_ref[...].astype(jnp.float32)
    d_out = (upstream * scale_ref[...]).astype(jnp.bfloat16)
    for block in range(4):
        cols = pl.ds(block * 256, 256)
        dact_ref[:, cols] = dot(d_out, wdown_ref[cols, :], ((1,), (1,)))
    need("centre", "counts", "paste", "kern", "gain", "wup", "paste_t", "cut_t")
    mine = lax.broadcasted_iota(jnp.int32, (4, tiles), 1) == tile
    keeps = jnp.sum(jnp.where(mine, counts_ref[...].astype(jnp.float32), 0.0), axis=1, keepdims=True)
    inner = dot(centre_ref[...], field_ref[...])
    dcp_ref[0:6] = jnp.zeros((6, SIDE, 256), jnp.float32)
    dcp_ref[WIDE : WIDE + 6] = jnp.zeros((6, SIDE, 256), jnp.float32)
    small_ref[...] = jnp.zeros((SMALL, 256), jnp.float32)
    for copy in copies:
        copy.wait_recv()
    for edge in range(4):
        turned[pl.ds(edge * PIECE, PIECE), :] = masked(got[lax.rem(edge + spin, 4)], edge)
    pad_ref[...] = (inner + dot(paste_ref[...], turned[...])).reshape(WIDE, PITCH, 256)
    for col in range(7):
        shift_ref[col] = pad_ref[:, pl.ds(col, SIDE), :]

    @pl.loop(0, SIDE // 4)
    def _(group):
        acc = [jnp.zeros((SIDE, 256), jnp.float32) for _ in range(4)]
        for col in range(7):
            for row in range(7):
                tap = kern_ref[row, pl.ds(col, 1), :]
                for line in range(4):
                    acc[line] = acc[line] + shift_ref[col, group * 4 + line + row] * tap
        for line in range(4):
            conv_ref[group * 4 + line] = acc[line]

    conv = conv_ref[...].reshape(SIDE * SIDE, 256)
    gain = gain_ref[...]
    centred = conv - jnp.mean(conv, axis=1, keepdims=True)
    inv_std = lax.rsqrt(jnp.mean(centred * centred, axis=1, keepdims=True) + epsilon)
    whitened = centred * inv_std
    normed = (whitened * gain).astype(jnp.bfloat16)
    projected = jnp.zeros((SIDE * SIDE, 256), jnp.float32)
    d_normed = jnp.zeros((SIDE * SIDE, 256), jnp.float32)
    per_part = 4 // PARTS
    for block in range(4):
        cols = pl.ds(block * 256, 256)
        part, local = block // per_part, block % per_part
        h = dot(normed, wup_ref[:, cols])
        square = h * h
        t = jnp.tanh(gelu_scale * h * (1.0 + gelu_cubic * square))
        half = 0.5 * (1.0 + t)
        activated = (h * half).astype(jnp.bfloat16)
        slope = half + 0.5 * h * (1.0 - t * t) * (gelu_scale * (1.0 + 3.0 * gelu_cubic * square))
        d_hidden = (dact_ref[:, cols] * slope).astype(jnp.bfloat16)
        gbuf[part, pl.ds(local * 512, 256)] = dot(normed, d_hidden, ((0,), (0,))).astype(jnp.bfloat16)
        gbuf[part, pl.ds(local * 512 + 256, 256)] = dot(activated, d_out, ((0,), (0,))).astype(jnp.bfloat16)
        if local == per_part - 1:
            begin(part)
        projected = projected + dot(activated, wdown_ref[cols, :])
        d_normed = d_normed + dot(d_hidden, wup_ref[:, cols], ((1,), (1,)))
    for part in range(PARTS - 1):
        advance(part)

    small_ref[49:50, :] = jnp.sum(d_normed * whitened, axis=0, keepdims=True)
    small_ref[50:51, :] = jnp.sum(upstream * projected, axis=0, keepdims=True)
    d_white = d_normed * gain
    d_conv = inv_std * (
        d_white
        - jnp.mean(d_white, axis=1, keepdims=True)
        - whitened * jnp.mean(d_white * whitened, axis=1, keepdims=True)
    )
    dcp_ref[6:WIDE] = d_conv.reshape(SIDE, SIDE, 256)
    advance(PARTS - 1)

    @pl.loop(0, WIDE // 2)
    def _(group):
        total = [jnp.zeros((PITCH, 256), jnp.float32) for _ in range(2)]
        for col in range(7):
            acc = [jnp.zeros((SIDE, 256), jnp.float32) for _ in range(2)]
            for row in range(7):
                tap = kern_ref[row, pl.ds(col, 1), :]
                for line in range(2):
                    acc[line] = acc[line] + dcp_ref[group * 2 + line + 6 - row] * tap
            for line in range(2):
                long = jnp.concatenate([acc[line], jnp.zeros((8, 256), jnp.float32)], axis=0)
                total[line] = total[line] + (pltpu.roll(long, col, 0) if col else long)
        for line in range(2):
            dpad_ref[group * 2 + line] = total[line]

    rounded = dpad_ref[...].reshape(WIDE * PITCH, 256).astype(jnp.bfloat16)
    back = dot(paste_t_ref[...], rounded).astype(jnp.bfloat16)
    for edge in range(4):
        pieces_b[edge] = masked(back[edge * PIECE : (edge + 1) * PIECE], edge)
    copies = trade(pieces_b, sent_b, got_b, spin)
    for part in range(PARTS):
        advance(part)

    for col in range(7):
        def line_sum(line, acc, col=col):
            grads = dcp_ref[line + 6]
            return tuple(acc[row] + shift_ref[col, line + row] * grads for row in range(7))

        sums = lax.fori_loop(
            0, SIDE, line_sum, tuple(jnp.zeros((SIDE, 256), jnp.float32) for _ in range(7))
        )
        for row in range(7):
            small_ref[pl.ds(row * 7 + col, 1), :] = jnp.sum(sums[row], axis=0, keepdims=True)

    def small_begin(phase):
        own = small_bufs[phase].at[place(phase)]
        own[...] = small_ref[...].astype(jnp.bfloat16)
        return [push(own, own, member(phase, ahead)[0]) for ahead in range(1, phases[phase][2])]

    def small_finish(phase, copies):
        for copy in copies:
            copy.wait_recv()
        total = small_bufs[phase][0].astype(jnp.float32)
        for slot in range(1, phases[phase][2]):
            total = total + small_bufs[phase][slot].astype(jnp.float32)
        small_ref[...] = total

    small_copies = small_begin(count - 1)
    for _ in range(count):
        for part in range(PARTS):
            advance(part)
    gathers = [gather(part, count - 1) for part in range(PARTS)]

    for copy in copies:
        copy.wait_recv()
    for edge in range(4):
        turned[pl.ds(edge * PIECE, PIECE), :] = got_b[lax.rem(edge + spin, 4)]
    inside = dpad_ref[3 : 3 + SIDE, 3 : 3 + SIDE, :].reshape(SIDE * SIDE, 256)
    home = dot(cut_t_ref[...], turned[...])
    grad_ref[...] = (upstream + inside + home).astype(jnp.bfloat16)

    for phase in range(count - 1, -1, -1):
        small_finish(phase, small_copies)
        if phase > 0:
            small_copies = small_begin(phase - 1)
        for part in range(PARTS):
            for copy in gathers[part]:
                copy.wait_recv()
            if phase > 0:
                gathers[part] = gather(part, phase - 1)
    for block in range(4):
        part, local = block // per_part, block % per_part
        gup_ref[:, pl.ds(block * 256, 256)] = agbuf[part, pl.ds(local * 512, 256)]
        gdown_ref[pl.ds(block * 256, 256), :] = agbuf[part, pl.ds(local * 512 + 256, 256)]
    gsmall_ref[...] = small_ref[...]
    for copy in started:
        copy.wait_send()


def finish_all(
    factor, grad_ref, gup_ref, gdown_ref, gsmall_ref,
    out_grad, out_kernel, out_gain, out_up, out_down, out_scale,
    kernel_f, gain_f, scale_f, up_f, down_f, sem,
):
    copies = []

    def write(src, dst):
        copy = pltpu.make_async_copy(src, dst, sem.at[len(copies)])
        copy.start()
        copies.append(copy)

    write(grad_ref, out_grad)
    for block in range(4):
        rows = pl.ds(block * 256, 256)
        down_f[rows] = gdown_ref[rows, :].astype(jnp.float32) * factor
        write(down_f.at[rows], out_down.at[rows])
    for block in range(4):
        rows = pl.ds(block * 64, 64)
        up_f[rows] = gup_ref[rows, :].astype(jnp.float32) * factor
        write(up_f.at[rows], out_up.at[rows])
    small = gsmall_ref[...] * factor
    for row in range(7):
        kernel_f[row] = small[row * 7 : row * 7 + 7]
    gain_f[...] = small[49:50]
    scale_f[...] = small[50:51]
    write(kernel_f, out_kernel)
    write(gain_f, out_gain)
    write(scale_f, out_scale)
    for copy in copies:
        copy.wait()


def on_device(tiles, reps, fields, upstream, kernel, gain, w_up, w_down, scale, spins, corner_counts):
    rows = 2048 // PARTS
    plans = [plan(tiles, reps, rows, part in BACKWARDS) for part in range(PARTS)]
    phases = plans[0]
    bf16, f32 = jnp.bfloat16, jnp.float32
    per_part = sum(size - 1 for _, _, size, _, _, _ in phases)
    sems = 16 + per_part * (2 * PARTS + 1)
    piece = pltpu.VMEM((4, PIECE, 256), bf16)
    vector = pltpu.VMEM
    scratch = [
        vector((SIDE * SIDE, 256), bf16), vector((SIDE * SIDE, 256), bf16),
        vector((7, 7, 256), f32), vector((1, 256), f32),
        vector((256, 1024), bf16), vector((1024, 256), bf16), vector((1, 256), f32),
        pltpu.SMEM((tiles,), jnp.int32), vector((4, tiles), jnp.int32),
        vector((4 * PIECE, SIDE * SIDE), bf16), vector((SIDE * SIDE, 4 * PIECE), bf16),
        vector((WIDE * PITCH, 4 * PIECE), bf16), vector((4 * PIECE, WIDE * PITCH), bf16),
        vector((WIDE * PITCH, SIDE * SIDE), bf16),
        pltpu.SemaphoreType.DMA((14,)),
        piece, piece, piece, piece, piece, piece,
        pltpu.VMEM((4 * PIECE, 256), bf16),
        pltpu.VMEM((WIDE, PITCH, 256), f32),
        pltpu.VMEM((7, WIDE, SIDE, 256), f32),
        pltpu.VMEM((SIDE, SIDE, 256), f32),
        pltpu.VMEM((SIDE * SIDE, 1024), f32),
        pltpu.VMEM((WIDE + 6, SIDE, 256), f32),
        pltpu.VMEM((WIDE, PITCH, 256), f32),
        pltpu.VMEM((PARTS, rows, 256), bf16),
        pltpu.VMEM((PARTS, rows, 256), bf16),
        pltpu.VMEM((SMALL, 256), f32),
        pltpu.SemaphoreType.DMA((sems,)),
        pltpu.SemaphoreType.DMA((sems,)),
    ]
    for ways in plans:
        for _, _, size, scatter, _, out in ways:
            scratch.append(pltpu.VMEM((size - 1 if scatter else size, out, 256), bf16))
    for ways in plans:
        for _, _, _, _, _, out in ways:
            scratch.append(pltpu.VMEM((out, 256), bf16))
    for _, _, size, _, _, _ in phases:
        scratch.append(pltpu.VMEM((size, SMALL, 256), bf16))
    vmem = pl.BlockSpec(memory_space=pltpu.VMEM)
    anywhere = pl.BlockSpec(memory_space=pltpu.HBM)
    grad, gup, gdown, gsmall = pl.pallas_call(
        functools.partial(body, tiles, plans),
        out_shape=[
            pltpu.VMEM((SIDE * SIDE, 256), bf16),
            pltpu.VMEM((256, 1024), bf16),
            pltpu.VMEM((1024, 256), bf16),
            pltpu.VMEM((SMALL, 256), f32),
        ],
        in_specs=[anywhere] * 14,
        out_specs=[vmem] * 4,
        scratch_shapes=scratch,
        compiler_params=pltpu.CompilerParams(
            collective_id=0, has_side_effects=True, vmem_limit_bytes=57 * 2**20
        ),
        cost_estimate=pl.CostEstimate(flops=10**9, bytes_accessed=8 * 2**20, transcendentals=2**18),
        name="block",
    )(
        fields.reshape(SIDE * SIDE, 256), upstream.reshape(SIDE * SIDE, 256),
        kernel, gain.reshape(1, 256), w_up, w_down, scale.reshape(1, 256),
        spins, corner_counts.T, *tables(),
    )
    factor = 1.0 / math.sqrt(tiles * reps * SIDE * SIDE)
    grad, kernel_grad, gain_grad, up_grad, down_grad, scale_grad = pl.pallas_call(
        functools.partial(finish_all, factor),
        out_shape=[
            jax.ShapeDtypeStruct((SIDE * SIDE, 256), bf16),
            jax.ShapeDtypeStruct((7, 7, 256), f32),
            jax.ShapeDtypeStruct((1, 256), f32),
            jax.ShapeDtypeStruct((256, 1024), f32),
            jax.ShapeDtypeStruct((1024, 256), f32),
            jax.ShapeDtypeStruct((1, 256), f32),
        ],
        in_specs=[vmem] * 4,
        out_specs=[anywhere] * 6,
        scratch_shapes=[
            pltpu.VMEM((7, 7, 256), f32), pltpu.VMEM((1, 256), f32), pltpu.VMEM((1, 256), f32),
            pltpu.VMEM((256, 1024), f32), pltpu.VMEM((1024, 256), f32),
            pltpu.SemaphoreType.DMA((12,)),
        ],
        compiler_params=pltpu.CompilerParams(vmem_limit_bytes=16 * 2**20),
        name="finish",
    )(grad, gup, gdown, gsmall)
    return (
        grad.reshape(fields.shape), kernel_grad, gain_grad.reshape(256),
        up_grad, down_grad, scale_grad.reshape(256),
    )


def solution(mesh):
    spread = P("rep", "tile", None, None, None)
    return jax.shard_map(
        functools.partial(on_device, mesh.shape["tile"], mesh.shape["rep"]),
        mesh=mesh,
        in_specs=(spread, spread) + (P(),) * 7,
        out_specs=(spread,) + (P(),) * 5,
        check_vma=False,
    )
```

```python
import functools
import math

import jax
import jax.numpy as jnp
import numpy as np
from jax import lax
from jax.experimental import pallas as pl
from jax.experimental.pallas import tpu as pltpu
from jax.sharding import PartitionSpec as P

epsilon = 1e-06
gelu_scale = 0.7978845608028654
gelu_cubic = 0.044715
MESH = pl.DeviceIdType.MESH
SIDE = 16
WIDE = 22
PITCH = 24
PIECE = 64
SMALL = 64
PARTS = 4
BACKWARDS = (0,)
ARGS = (
    "field", "up", "kern", "gain", "wup", "wdown", "scale", "spins", "counts",
    "cut", "cut_t", "paste", "paste_t", "centre",
)
LOADS = (
    "field", "cut", "spins", "up", "scale", "wdown", "centre", "counts", "paste", "kern",
    "gain", "wup", "paste_t", "cut_t",
)


def tables():
    cells = np.arange(SIDE * SIDE).reshape(SIDE, SIDE)
    pads = np.arange(WIDE * PITCH).reshape(WIDE, PITCH)[:, :WIDE]
    cut = np.zeros((4 * PIECE, SIDE * SIDE), np.float32)
    paste = np.zeros((WIDE * PITCH, 4 * PIECE), np.float32)
    centre = np.zeros((WIDE * PITCH, SIDE * SIDE), np.float32)
    for edge in range(4):
        turned = np.rot90(cells, edge)
        wide = np.rot90(pads, edge)
        for depth in range(3):
            for along in range(SIDE):
                cut[edge * PIECE + depth * SIDE + along, turned[depth, along]] = 1
                paste[wide[2 - depth, 3 + along], edge * PIECE + depth * SIDE + SIDE - 1 - along] = 1
            for along in range(3):
                row = edge * PIECE + 48 + depth * 3 + along
                cut[row, turned[depth, along]] = 1
                paste[wide[2 - depth, 2 - along], row] = 1
    for row in range(SIDE):
        for col in range(SIDE):
            centre[pads[row + 3, col + 3], cells[row, col]] = 1
    return [jnp.asarray(t, jnp.bfloat16) for t in (cut, cut.T, paste, paste.T, centre)]


def plan(tiles, reps, rows, backwards=False):
    groups = []
    if reps > 1:
        groups.append(("rep", 1, reps))
    stride = 1
    while stride < tiles:
        size = 4 if tiles // stride % 4 == 0 else 2
        groups.append(("tile", stride, size))
        stride *= size
    if backwards:
        groups = [g for g in groups if g[0] == "rep"] + [g for g in groups if g[0] != "rep"][::-1]
    phases = []
    for axis, stride, size in groups:
        scatter = rows % (16 * size) == 0
        out = rows // size if scatter else rows
        phases.append((axis, stride, size, scatter, rows, out))
        rows = out
    return phases


def dot(left, right, dims=((1,), (0,))):
    return lax.dot_general(left, right, (dims, ((), ())), preferred_element_type=jnp.float32)


def body(
    tiles, plans,
    *refs,
):
    sources, refs = refs[:14], refs[14:]
    outputs, refs = refs[:4], refs[4:]
    held, load_sem, refs = refs[:14], refs[14], refs[15:]
    loads = {}
    for name in LOADS:
        slot = ARGS.index(name)
        loads[name] = pltpu.make_async_copy(sources[slot], held[slot], load_sem.at[slot])
        loads[name].start()

    def need(*names):
        for name in names:
            loads[name].wait()

    work(tiles, plans, need, *held, *outputs, *refs)


def work(
    tiles, plans, need,
    field_ref, up_ref, kern_ref, gain_ref, wup_ref, wdown_ref, scale_ref, spins_ref, counts_ref,
    cut_ref, cut_t_ref, paste_ref, paste_t_ref, centre_ref,
    grad_ref, gup_ref, gdown_ref, gsmall_ref,
    pieces, sent, got, pieces_b, sent_b, got_b, turned,
    pad_ref, shift_ref, conv_ref, dact_ref, dcp_ref, dpad_ref, gbuf, agbuf, small_ref,
    send_sem, recv_sem, *bufs,
):
    phases = plans[-1]
    count = len(phases)
    recv_bufs = [bufs[part * count : (part + 1) * count] for part in range(PARTS)]
    bufs = bufs[PARTS * count :]
    red_bufs = [bufs[part * count : (part + 1) * count] for part in range(PARTS)]
    small_bufs = bufs[PARTS * count :]
    tile = lax.axis_index("tile")
    rep = lax.axis_index("rep")
    side = tiles // 2 ** ((tiles.bit_length() - 1) // 2)
    steps = [-side, 1, side, -1, -side - 1, -side + 1, side + 1, side - 1]

    def across(step):
        return {"tile": lax.rem(tile + step + tiles, tiles)}

    def place(phase, phases=phases):
        axis, stride, size = phases[phase][:3]
        return rep if axis == "rep" else lax.rem(tile // stride, size)

    def member(phase, ahead, phases=phases):
        axis, stride, size = phases[phase][:3]
        pos = place(phase, phases)
        other = lax.rem(pos + ahead, size)
        if axis == "rep":
            return {"rep": other}, other
        return {"tile": tile + (other - pos) * stride}, other

    barrier = pltpu.get_barrier_semaphore()
    greeted = 0
    for step in steps:
        pl.semaphore_signal(barrier, inc=1, device_id=across(step), device_id_type=MESH)
        greeted += 1
    for phase in range(count):
        for ahead in range(1, phases[phase][2]):
            pl.semaphore_signal(
                barrier, inc=1, device_id=member(phase, ahead)[0], device_id_type=MESH
            )
            greeted += 1

    used = [0]
    started = []

    def push(src, dst, device):
        slot = used[0]
        used[0] += 1
        copy = pltpu.make_async_remote_copy(
            src_ref=src, dst_ref=dst, send_sem=send_sem.at[slot], recv_sem=recv_sem.at[slot],
            device_id=device, device_id_type=MESH,
        )
        copy.start()
        started.append(copy)
        return copy

    is_corner = lax.broadcasted_iota(jnp.int32, (PIECE, 256), 0) >= 48

    def masked(piece, edge):
        keep = jnp.where(is_corner, keeps[edge : edge + 1, :], 1.0)
        return (piece.astype(jnp.float32) * keep).astype(jnp.bfloat16)

    def trade(source, out, into, spin):
        for grid in range(4):
            out[grid] = source[lax.rem(grid - spin + 4, 4)]
        copies = []
        for grid in range(4):
            copies.append(push(out.at[grid, pl.ds(0, 48)], into.at[(grid + 2) % 4, pl.ds(0, 48)], across(steps[grid])))
        for grid in range(4):
            copies.append(push(out.at[grid, pl.ds(48, 16)], into.at[(grid + 2) % 4, pl.ds(48, 16)], across(steps[4 + grid])))
        return copies

    flying = [None] * PARTS
    reached = [0] * PARTS
    offsets = []
    for ways in plans:
        offset = 0
        offsets.append([])
        for phase in range(count):
            if ways[phase][3]:
                offset = offset + place(phase, ways) * ways[phase][5]
            offsets[-1].append(offset)

    def source_of(part, phase):
        return gbuf.at[part] if phase == 0 else red_bufs[part][phase - 1]

    def begin(part):
        phase, ways = reached[part], plans[part]
        size, scatter, rows, out = ways[phase][2:]
        src = source_of(part, phase)
        copies = []
        if not scatter:
            recv_bufs[part][phase][place(phase, ways)] = src[...]
        for ahead in range(1, size):
            device, other = member(phase, ahead, ways)
            if scatter:
                start = pl.multiple_of(other * out, 16)
                copies.append(push(src.at[pl.ds(start, out)], recv_bufs[part][phase].at[ahead - 1], device))
            else:
                copies.append(push(src, recv_bufs[part][phase].at[place(phase, ways)], device))
        flying[part] = copies

    def finish(part):
        phase, ways = reached[part], plans[part]
        size, scatter, rows, out = ways[phase][2:]
        src = source_of(part, phase)
        for copy in flying[part]:
            copy.wait_recv()
        if scatter:
            total = src[pl.ds(pl.multiple_of(place(phase, ways) * out, 16), out)].astype(jnp.float32)
            for slot in range(size - 1):
                total = total + recv_bufs[part][phase][slot].astype(jnp.float32)
        else:
            total = recv_bufs[part][phase][0].astype(jnp.float32)
            for slot in range(1, size):
                total = total + recv_bufs[part][phase][slot].astype(jnp.float32)
        reached[part] += 1
        if reached[part] < count:
            red_bufs[part][phase][...] = total.astype(jnp.bfloat16)
        else:
            agbuf[part, pl.ds(pl.multiple_of(offsets[part][-1], 16), out)] = total.astype(jnp.bfloat16)

    def advance(part):
        if reached[part] < count:
            finish(part)
            if reached[part] < count:
                begin(part)

    def gather(part, phase):
        ways = plans[part]
        size, scatter, rows, out = ways[phase][2:]
        if not scatter:
            return []
        here = agbuf.at[part, pl.ds(pl.multiple_of(offsets[part][phase], 16), out)]
        return [push(here, here, member(phase, ahead, ways)[0]) for ahead in range(1, size)]

    need("field", "cut", "spins")
    spin = spins_ref[tile]
    pieces[...] = dot(cut_ref[...], field_ref[...]).astype(jnp.bfloat16).reshape(4, PIECE, 256)
    pl.semaphore_wait(barrier, greeted)
    copies = trade(pieces, sent, got, spin)
    need("up", "scale", "wdown")
    upstream = up_ref[...].astype(jnp.float32)
    d_out = (upstream * scale_ref[...]).astype(jnp.bfloat16)
    for block in range(4):
        cols = pl.ds(block * 256, 256)
        dact_ref[:, cols] = dot(d_out, wdown_ref[cols, :], ((1,), (1,)))
    need("centre", "counts", "paste", "kern", "gain", "wup", "paste_t", "cut_t")
    mine = lax.broadcasted_iota(jnp.int32, (4, tiles), 1) == tile
    keeps = jnp.sum(jnp.where(mine, counts_ref[...].astype(jnp.float32), 0.0), axis=1, keepdims=True)
    inner = dot(centre_ref[...], field_ref[...])
    dcp_ref[0:6] = jnp.zeros((6, SIDE, 256), jnp.float32)
    dcp_ref[WIDE : WIDE + 6] = jnp.zeros((6, SIDE, 256), jnp.float32)
    small_ref[...] = jnp.zeros((SMALL, 256), jnp.float32)
    for copy in copies:
        copy.wait_recv()
    for edge in range(4):
        turned[pl.ds(edge * PIECE, PIECE), :] = masked(got[lax.rem(edge + spin, 4)], edge)
    pad_ref[...] = (inner + dot(paste_ref[...], turned[...])).reshape(WIDE, PITCH, 256)
    for col in range(7):
        shift_ref[col] = pad_ref[:, pl.ds(col, SIDE), :]

    @pl.loop(0, SIDE // 4)
    def _(group):
        acc = [jnp.zeros((SIDE, 256), jnp.float32) for _ in range(4)]
        for col in range(7):
            for row in range(7):
                tap = kern_ref[row, pl.ds(col, 1), :]
                for line in range(4):
                    acc[line] = acc[line] + shift_ref[col, group * 4 + line + row] * tap
        for line in range(4):
            conv_ref[group * 4 + line] = acc[line]

    conv = conv_ref[...].reshape(SIDE * SIDE, 256)
    gain = gain_ref[...]
    centred = conv - jnp.mean(conv, axis=1, keepdims=True)
    inv_std = lax.rsqrt(jnp.mean(centred * centred, axis=1, keepdims=True) + epsilon)
    whitened = centred * inv_std
    normed = (whitened * gain).astype(jnp.bfloat16)
    projected = jnp.zeros((SIDE * SIDE, 256), jnp.float32)
    d_normed = jnp.zeros((SIDE * SIDE, 256), jnp.float32)
    per_part = 4 // PARTS
    for block in range(4):
        cols = pl.ds(block * 256, 256)
        part, local = block // per_part, block % per_part
        h = dot(normed, wup_ref[:, cols])
        square = h * h
        t = jnp.tanh(gelu_scale * h * (1.0 + gelu_cubic * square))
        half = 0.5 * (1.0 + t)
        activated = (h * half).astype(jnp.bfloat16)
        slope = half + 0.5 * h * (1.0 - t * t) * (gelu_scale * (1.0 + 3.0 * gelu_cubic * square))
        d_hidden = (dact_ref[:, cols] * slope).astype(jnp.bfloat16)
        gbuf[part, pl.ds(local * 512, 256)] = dot(normed, d_hidden, ((0,), (0,))).astype(jnp.bfloat16)
        gbuf[part, pl.ds(local * 512 + 256, 256)] = dot(activated, d_out, ((0,), (0,))).astype(jnp.bfloat16)
        if local == per_part - 1:
            begin(part)
        projected = projected + dot(activated, wdown_ref[cols, :])
        d_normed = d_normed + dot(d_hidden, wup_ref[:, cols], ((1,), (1,)))
    for part in range(PARTS - 1):
        advance(part)

    small_ref[49:50, :] = jnp.sum(d_normed * whitened, axis=0, keepdims=True)
    small_ref[50:51, :] = jnp.sum(upstream * projected, axis=0, keepdims=True)
    d_white = d_normed * gain
    d_conv = inv_std * (
        d_white
        - jnp.mean(d_white, axis=1, keepdims=True)
        - whitened * jnp.mean(d_white * whitened, axis=1, keepdims=True)
    )
    dcp_ref[6:WIDE] = d_conv.reshape(SIDE, SIDE, 256)
    advance(PARTS - 1)

    @pl.loop(0, WIDE // 2)
    def _(group):
        total = [jnp.zeros((PITCH, 256), jnp.float32) for _ in range(2)]
        for col in range(7):
            acc = [jnp.zeros((SIDE, 256), jnp.float32) for _ in range(2)]
            for row in range(7):
                tap = kern_ref[row, pl.ds(col, 1), :]
                for line in range(2):
                    acc[line] = acc[line] + dcp_ref[group * 2 + line + 6 - row] * tap
            for line in range(2):
                long = jnp.concatenate([acc[line], jnp.zeros((8, 256), jnp.float32)], axis=0)
                total[line] = total[line] + (pltpu.roll(long, col, 0) if col else long)
        for line in range(2):
            dpad_ref[group * 2 + line] = total[line]

    rounded = dpad_ref[...].reshape(WIDE * PITCH, 256).astype(jnp.bfloat16)
    back = dot(paste_t_ref[...], rounded).astype(jnp.bfloat16)
    for edge in range(4):
        pieces_b[edge] = masked(back[edge * PIECE : (edge + 1) * PIECE], edge)
    copies = trade(pieces_b, sent_b, got_b, spin)
    for part in range(PARTS):
        advance(part)

    for col in range(7):
        def line_sum(line, acc, col=col):
            grads = dcp_ref[line + 6]
            return tuple(acc[row] + shift_ref[col, line + row] * grads for row in range(7))

        sums = lax.fori_loop(
            0, SIDE, line_sum, tuple(jnp.zeros((SIDE, 256), jnp.float32) for _ in range(7))
        )
        for row in range(7):
            small_ref[pl.ds(row * 7 + col, 1), :] = jnp.sum(sums[row], axis=0, keepdims=True)

    def small_begin(phase):
        own = small_bufs[phase].at[place(phase)]
        own[...] = small_ref[...].astype(jnp.bfloat16)
        return [push(own, own, member(phase, ahead)[0]) for ahead in range(1, phases[phase][2])]

    def small_finish(phase, copies):
        for copy in copies:
            copy.wait_recv()
        total = small_bufs[phase][0].astype(jnp.float32)
        for slot in range(1, phases[phase][2]):
            total = total + small_bufs[phase][slot].astype(jnp.float32)
        small_ref[...] = total

    small_copies = small_begin(count - 1)
    for _ in range(count):
        for part in range(PARTS):
            advance(part)
    gathers = [gather(part, count - 1) for part in range(PARTS)]

    for copy in copies:
        copy.wait_recv()
    for edge in range(4):
        turned[pl.ds(edge * PIECE, PIECE), :] = got_b[lax.rem(edge + spin, 4)]
    inside = dpad_ref[3 : 3 + SIDE, 3 : 3 + SIDE, :].reshape(SIDE * SIDE, 256)
    home = dot(cut_t_ref[...], turned[...])
    grad_ref[...] = (upstream + inside + home).astype(jnp.bfloat16)

    for phase in range(count - 1, -1, -1):
        small_finish(phase, small_copies)
        if phase > 0:
            small_copies = small_begin(phase - 1)
        for part in range(PARTS):
            for copy in gathers[part]:
                copy.wait_recv()
            if phase > 0:
                gathers[part] = gather(part, phase - 1)
    for block in range(4):
        part, local = block // per_part, block % per_part
        gup_ref[:, pl.ds(block * 256, 256)] = agbuf[part, pl.ds(local * 512, 256)]
        gdown_ref[pl.ds(block * 256, 256), :] = agbuf[part, pl.ds(local * 512 + 256, 256)]
    gsmall_ref[...] = small_ref[...]
    for copy in started:
        copy.wait_send()


def finish_all(
    factor, grad_ref, gup_ref, gdown_ref, gsmall_ref,
    out_grad, out_kernel, out_gain, out_up, out_down, out_scale,
    kernel_f, gain_f, scale_f, up_f, down_f, sem,
):
    copies = []

    def write(src, dst):
        copy = pltpu.make_async_copy(src, dst, sem.at[len(copies)])
        copy.start()
        copies.append(copy)

    write(grad_ref, out_grad)
    for block in range(4):
        rows = pl.ds(block * 256, 256)
        down_f[rows] = gdown_ref[rows, :].astype(jnp.float32) * factor
        write(down_f.at[rows], out_down.at[rows])
    for block in range(4):
        rows = pl.ds(block * 64, 64)
        up_f[rows] = gup_ref[rows, :].astype(jnp.float32) * factor
        write(up_f.at[rows], out_up.at[rows])
    small = gsmall_ref[...] * factor
    for row in range(7):
        kernel_f[row] = small[row * 7 : row * 7 + 7]
    gain_f[...] = small[49:50]
    scale_f[...] = small[50:51]
    write(kernel_f, out_kernel)
    write(gain_f, out_gain)
    write(scale_f, out_scale)
    for copy in copies:
        copy.wait()


def on_device(tiles, reps, fields, upstream, kernel, gain, w_up, w_down, scale, spins, corner_counts):
    rows = 2048 // PARTS
    plans = [plan(tiles, reps, rows, part in BACKWARDS) for part in range(PARTS)]
    phases = plans[-1]
    bf16, f32 = jnp.bfloat16, jnp.float32
    per_part = sum(size - 1 for _, _, size, _, _, _ in phases)
    sems = 16 + per_part * (2 * PARTS + 1)
    piece = pltpu.VMEM((4, PIECE, 256), bf16)
    vector = pltpu.VMEM
    scratch = [
        vector((SIDE * SIDE, 256), bf16), vector((SIDE * SIDE, 256), bf16),
        vector((7, 7, 256), f32), vector((1, 256), f32),
        vector((256, 1024), bf16), vector((1024, 256), bf16), vector((1, 256), f32),
        pltpu.SMEM((tiles,), jnp.int32), vector((4, tiles), jnp.int32),
        vector((4 * PIECE, SIDE * SIDE), bf16), vector((SIDE * SIDE, 4 * PIECE), bf16),
        vector((WIDE * PITCH, 4 * PIECE), bf16), vector((4 * PIECE, WIDE * PITCH), bf16),
        vector((WIDE * PITCH, SIDE * SIDE), bf16),
        pltpu.SemaphoreType.DMA((14,)),
        piece, piece, piece, piece, piece, piece,
        pltpu.VMEM((4 * PIECE, 256), bf16),
        pltpu.VMEM((WIDE, PITCH, 256), f32),
        pltpu.VMEM((7, WIDE, SIDE, 256), f32),
        pltpu.VMEM((SIDE, SIDE, 256), f32),
        pltpu.VMEM((SIDE * SIDE, 1024), f32),
        pltpu.VMEM((WIDE + 6, SIDE, 256), f32),
        pltpu.VMEM((WIDE, PITCH, 256), f32),
        pltpu.VMEM((PARTS, rows, 256), bf16),
        pltpu.VMEM((PARTS, rows, 256), bf16),
        pltpu.VMEM((SMALL, 256), f32),
        pltpu.SemaphoreType.DMA((sems,)),
        pltpu.SemaphoreType.DMA((sems,)),
    ]
    for ways in plans:
        for _, _, size, scatter, _, out in ways:
            scratch.append(pltpu.VMEM((size - 1 if scatter else size, out, 256), bf16))
    for ways in plans:
        for _, _, _, _, _, out in ways:
            scratch.append(pltpu.VMEM((out, 256), bf16))
    for _, _, size, _, _, _ in phases:
        scratch.append(pltpu.VMEM((size, SMALL, 256), bf16))
    vmem = pl.BlockSpec(memory_space=pltpu.VMEM)
    anywhere = pl.BlockSpec(memory_space=pltpu.HBM)
    grad, gup, gdown, gsmall = pl.pallas_call(
        functools.partial(body, tiles, plans),
        out_shape=[
            pltpu.VMEM((SIDE * SIDE, 256), bf16),
            pltpu.VMEM((256, 1024), bf16),
            pltpu.VMEM((1024, 256), bf16),
            pltpu.VMEM((SMALL, 256), f32),
        ],
        in_specs=[anywhere] * 14,
        out_specs=[vmem] * 4,
        scratch_shapes=scratch,
        compiler_params=pltpu.CompilerParams(
            collective_id=0, has_side_effects=True, vmem_limit_bytes=57 * 2**20
        ),
        cost_estimate=pl.CostEstimate(flops=10**9, bytes_accessed=8 * 2**20, transcendentals=2**18),
        name="block",
    )(
        fields.reshape(SIDE * SIDE, 256), upstream.reshape(SIDE * SIDE, 256),
        kernel, gain.reshape(1, 256), w_up, w_down, scale.reshape(1, 256),
        spins, corner_counts.T, *tables(),
    )
    factor = 1.0 / math.sqrt(tiles * reps * SIDE * SIDE)
    grad, kernel_grad, gain_grad, up_grad, down_grad, scale_grad = pl.pallas_call(
        functools.partial(finish_all, factor),
        out_shape=[
            jax.ShapeDtypeStruct((SIDE * SIDE, 256), bf16),
            jax.ShapeDtypeStruct((7, 7, 256), f32),
            jax.ShapeDtypeStruct((1, 256), f32),
            jax.ShapeDtypeStruct((256, 1024), f32),
            jax.ShapeDtypeStruct((1024, 256), f32),
            jax.ShapeDtypeStruct((1, 256), f32),
        ],
        in_specs=[vmem] * 4,
        out_specs=[anywhere] * 6,
        scratch_shapes=[
            pltpu.VMEM((7, 7, 256), f32), pltpu.VMEM((1, 256), f32), pltpu.VMEM((1, 256), f32),
            pltpu.VMEM((256, 1024), f32), pltpu.VMEM((1024, 256), f32),
            pltpu.SemaphoreType.DMA((12,)),
        ],
        compiler_params=pltpu.CompilerParams(vmem_limit_bytes=16 * 2**20),
        name="finish",
    )(grad, gup, gdown, gsmall)
    return (
        grad.reshape(fields.shape), kernel_grad, gain_grad.reshape(256),
        up_grad, down_grad, scale_grad.reshape(256),
    )


def solution(mesh):
    spread = P("rep", "tile", None, None, None)
    return jax.shard_map(
        functools.partial(on_device, mesh.shape["tile"], mesh.shape["rep"]),
        mesh=mesh,
        in_specs=(spread, spread) + (P(),) * 7,
        out_specs=(spread,) + (P(),) * 5,
        check_vma=False,
    )
```
